32 devices in a mesh: wave: 32 (over z, y, x, core), lev: 1.
Axes of the slice: x: 2, y: 2, z: 4, core: 2. Of those that a mesh axis runs over, the one named last changes fastest.
Arguments:
- fourier: bfloat16 [2560, 16, 4, 128], P('wave', 'lev'), may hold values from -6 to 6
- owner: int32 [64], replicated, may hold values from 0 to 63, each once
- legendre: bfloat16 [64, 2, 640, 1280], P('wave'), may hold values from -0.125 to 0.125
- quad_weights: float32 [1280], replicated, may hold values from 0.5 to 2
- layer_depth: float32 [16], P('lev'), may hold values from 0.05 to 0.3
Outputs:
- fields_out: bfloat16 [2560, 16, 4, 128], P('wave', 'lev')
- geopotential: bfloat16 [2560, 16, 128], P('wave', 'lev')
The draws below stay inside these ranges and needn't reach their ends.
Inputs may be any that keep to these rules, and one draw needn't show every extreme that they name: owner is a permutation of the slots; slot s lies on index s // 2 of wave.
All inputs are finite; a program needn't handle non-finite values.
Results may differ from the reference program's by a relative error of at most 0.0063.
Values may be sent and summed in bfloat16 or wider, within the bound.
A program may use at most 64 MiB of HBM per device.

```python
import math
import jax
import jax.numpy as jnp
from jax import lax

NMAX = 1280
NLATH = 1280
FIELDS = 4
LEV = 16
MW = 64
NLAT = 2560
HALF = 640


def shard_levels(rng, dims, split, smallest, top_value):
    gain, own = 1.0, jax.random.fold_in(rng, 6)
    for position, blocks in split:
        heights = jnp.exp(jax.random.uniform(jax.random.fold_in(own, position), (blocks,), jnp.float32, smallest / len(split), top_value / len(split)))
        gain = gain * jnp.repeat(heights, dims[position] // blocks).reshape([-1 if axis == position else 1 for axis in range(len(dims))])
    return gain


def gaussian(own_key, extent, width, bound, cuts=(), kind=jnp.bfloat16):
    entries = jax.random.normal(own_key, extent, jnp.float32) * width
    if len(cuts) > 0:
        entries = shard_levels(own_key, extent, cuts, -0.22, 0.18) * entries
    return jnp.clip(entries, min=-bound, max=bound).astype(kind)


def setup_inputs(seed: int = 0) -> dict:
    seeds = jax.random.split(jax.random.key(seed), 6)
    fourier = gaussian(seeds[0], (NLAT, LEV, FIELDS, 2 * MW), 1.0, 6.0, ((0, 32),))
    owner = jax.random.permutation(seeds[1], MW).astype(jnp.int32)
    legendre = gaussian(seeds[2], (MW, 2, HALF, NLATH), NLAT ** -0.5, 0.125, ((0, 32),))
    quad_weights = jnp.clip(jnp.exp(jax.random.uniform(seeds[3], (NLATH,), jnp.float32, math.log(0.5), math.log(2.0))), 0.5, 2.0)
    layer_depth = jnp.clip(jnp.exp(jax.random.uniform(seeds[4], (LEV,), jnp.float32, math.log(0.05), math.log(0.3))), 0.05, 0.3)
    return dict(fourier=fourier, owner=owner, legendre=legendre, quad_weights=quad_weights, layer_depth=layer_depth)


def reference(fourier, owner, legendre, quad_weights, layer_depth):
    unpacked = fourier.reshape(NLAT, LEV, FIELDS, 2, MW)
    columns_all = jnp.transpose(unpacked, (4, 0, 1, 2, 3)).reshape(MW, NLAT, LEV * FIELDS * 2)
    degree_rows = jnp.arange(HALF, dtype=jnp.int32)

    def transform(inputs):
        wave_index, columns = inputs
        tables = legendre[owner[wave_index]]
        length = NMAX - (wave_index * NMAX) // MW
        values = columns.astype(jnp.float32)
        northern = values[:NLATH]
        southern = values[NLATH:][::-1]
        scaled = quad_weights[:, None]
        folded = ((scaled * (northern + southern)).astype(jnp.bfloat16),
                  (scaled * (northern - southern)).astype(jnp.bfloat16))
        halves = []
        for parity in range(2):
            spectra = jnp.dot(tables[parity], folded[parity], preferred_element_type=jnp.float32)
            living = (2 * degree_rows + parity) < length
            spectra = jnp.where(living[:, None], spectra, jnp.float32(0.0)).astype(jnp.bfloat16)
            halves.append(jnp.dot(tables[parity].T, spectra, preferred_element_type=jnp.float32))
        upper = halves[0] + halves[1]
        lower = halves[0] - halves[1]
        return jnp.concatenate([upper, lower[::-1]], axis=0).astype(jnp.bfloat16)

    results = lax.map(transform, (jnp.arange(MW, dtype=jnp.int32), columns_all))
    fields_out = jnp.transpose(results.reshape(MW, NLAT, LEV, FIELDS, 2), (1, 2, 3, 4, 0)).reshape(NLAT, LEV, FIELDS, 2 * MW)
    contrib = layer_depth[None, :, None] * fields_out[:, :, 0, :].astype(jnp.float32)
    inclusive = jnp.cumsum(contrib[:, ::-1], axis=1)[:, ::-1]
    geopotential = (inclusive - 0.5 * contrib).astype(jnp.bfloat16)
    return fields_out, geopotential
```

```python
import functools

import jax
import jax.numpy as jnp
from jax import lax
from jax.experimental import pallas as pl
from jax.experimental.pallas import tpu as pltpu
from jax.sharding import PartitionSpec as P

MESH = pl.DeviceIdType.MESH
GROUP = 16
NT = (((1,), (1,)), ((), ()))
TN = (((0,), (0,)), ((), ()))


def kernel(
    n,
    slots,
    degrees,
    x_ref,
    own_ref,
    depth_ref,
    weight_ref,
    table_hbm,
    out_ref,
    geo_ref,
    tables,
    outgoing,
    arrived,
    weights,
    folded,
    spectra,
    results,
    returned,
    table_sem,
    send_sem,
    recv_sem,
    own_sem,
):
    me = lax.axis_index("wave")
    lats, lf, lanes = x_ref.shape
    waves = n * slots
    half = tables.shape[2]
    north = tables.shape[3]
    whole = n * lats
    levels = geo_ref.shape[1]
    fields = lf // levels

    barrier = pltpu.get_barrier_semaphore()

    def greet(step, carry):
        other = lax.rem(me + step, n)
        pl.semaphore_signal(barrier, inc=1, device_id={"wave": other}, device_id_type=MESH)
        return carry

    lax.fori_loop(1, n, greet, 0)

    def table_copy(slot):
        return pltpu.make_async_copy(table_hbm.at[slot], tables.at[slot], table_sem.at[slot])

    for slot in range(slots):
        table_copy(slot).start()

    south = me >= n // 2
    place = jnp.where(south, n // 2 + (n - 1 - me), me)

    def lat_of(turn):
        return jnp.where(south, lats - 1 - turn, turn)

    rows_i = lax.broadcasted_iota(jnp.int32, (lanes, lanes), 0)
    permute = jnp.where(rows_i == own_ref[...], 1.0, 0.0).astype(jnp.bfloat16)
    low = lax.broadcasted_iota(jnp.int32, (waves, lanes), 1) < lf

    def scatter_group(group, carry):
        parts = []
        for pair in range(GROUP // 2):
            turn = group * GROUP + 2 * pair
            two = jnp.concatenate([x_ref[lat_of(turn)], x_ref[lat_of(turn + 1)]], axis=0)
            mixed = lax.dot_general(permute, two, NT, preferred_element_type=jnp.float32)
            real, imag = mixed[:waves], mixed[waves:]
            parts.append(jnp.where(low, real, pltpu.roll(imag, lf, 1)))
            parts.append(jnp.where(low, pltpu.roll(real, lf, 1), imag))
        block = jnp.swapaxes(jnp.stack(parts, axis=0), 0, 1)
        start = pl.multiple_of(group * GROUP, GROUP)
        outgoing[:, pl.ds(start, GROUP), :] = block.astype(jnp.bfloat16)
        return carry

    lax.fori_loop(0, lats // GROUP, scatter_group, 0)
    pl.semaphore_wait(barrier, n - 1)

    def rows(ref, start, count):
        return ref.at[pl.ds(pl.multiple_of(start, GROUP), count), :]

    def partner(turn):
        return lax.rem(
            me + jnp.where(lax.rem(turn, 2) == 0, n // 2 + turn // 2, (turn + 1) // 2), n
        )

    def send_out(slot):
        target = rows(arrived, slot * whole + place * lats, lats)

        def one(turn, carry):
            other = partner(turn)
            pltpu.make_async_remote_copy(
                src_ref=outgoing.at[other * slots + slot],
                dst_ref=target,
                send_sem=send_sem.at[0, slot],
                recv_sem=recv_sem.at[0, slot],
                device_id={"wave": other},
                device_id_type=MESH,
            ).start()
            return carry

        lax.fori_loop(0, n - 1, one, 0)
        own_out(slot).start()

    def own_out(slot):
        return pltpu.make_async_copy(
            outgoing.at[me * slots + slot],
            rows(arrived, slot * whole + place * lats, lats),
            own_sem.at[0, slot],
        )

    def place_of(other):
        return jnp.where(other >= n // 2, n // 2 + (n - 1 - other), other)

    def send_back(slot):
        def one(turn, carry):
            other = partner(turn)
            pltpu.make_async_remote_copy(
                src_ref=rows(results, slot * whole + place_of(other) * lats, lats),
                dst_ref=returned.at[me * slots + slot],
                send_sem=send_sem.at[1, slot],
                recv_sem=recv_sem.at[1, slot],
                device_id={"wave": other},
                device_id_type=MESH,
            ).start()
            return carry

        lax.fori_loop(0, n - 1, one, 0)
        own_back(slot).start()

    def own_back(slot):
        return pltpu.make_async_copy(
            rows(results, slot * whole + place * lats, lats),
            returned.at[me * slots + slot],
            own_sem.at[1, slot],
        )

    def all_of(ref, sem):
        return pltpu.make_async_copy(ref, ref, sem)

    many = (n - 1) * lats
    for slot in range(slots):
        send_out(slot)

    for group in range(north // lanes):
        row = weight_ref[group : group + 1, :]
        weights[group * lanes : (group + 1) * lanes, :] = jnp.transpose(
            jnp.broadcast_to(row, (lanes, lanes))
        )

    lane = lax.broadcasted_iota(jnp.int32, (1, lanes), 1)
    lengths = degrees - (lane * degrees) // waves
    span = 2 * lanes
    part = lanes

    for slot in range(slots):
        table_copy(slot).wait()
        own_out(slot).wait()
        all_of(rows(arrived, slot * whole, many), recv_sem.at[0, slot]).wait()

        def fold(index, carry, slot=slot):
            start = pl.multiple_of(index * span, span)
            upper = arrived[pl.ds(slot * whole + start, span), :].astype(jnp.float32)
            lower = arrived[pl.ds(slot * whole + north + start, span), :].astype(jnp.float32)
            scale = weights[pl.ds(start, span), :]
            folded[0, pl.ds(start, span), :] = (scale * (upper + lower)).astype(jnp.bfloat16)
            folded[1, pl.ds(start, span), :] = (scale * (upper - lower)).astype(jnp.bfloat16)
            return carry

        lax.fori_loop(0, north // span, fold, 0)
        mine = (own_ref[...] == me * slots + slot) & (lane < waves)
        length = jnp.sum(jnp.where(mine, lengths, 0), axis=1, keepdims=True)

        def direct(index, carry, slot=slot, length=length):
            start = pl.multiple_of(index * part, part)
            degree = 2 * (start + lax.broadcasted_iota(jnp.int32, (part, lanes), 0))
            for parity in range(2):
                value = jnp.dot(
                    tables[slot, parity, pl.ds(start, part), :],
                    folded[parity],
                    preferred_element_type=jnp.float32,
                )
                value = jnp.where(degree + parity < length, value, 0.0)
                spectra[parity, pl.ds(start, part), :] = value.astype(jnp.bfloat16)
            return carry

        lax.fori_loop(0, half // part, direct, 0)

        def inverse(index, carry, slot=slot):
            start = pl.multiple_of(index * span, span)
            even, odd = (
                lax.dot_general(
                    tables[slot, parity, :, pl.ds(start, span)],
                    spectra[parity],
                    TN,
                    preferred_element_type=jnp.float32,
                )
                for parity in range(2)
            )
            results[pl.ds(slot * whole + start, span), :] = (even + odd).astype(jnp.bfloat16)
            results[pl.ds(slot * whole + north + start, span), :] = (even - odd).astype(
                jnp.bfloat16
            )
            return carry

        lax.fori_loop(0, north // span, inverse, 0)
        send_back(slot)

    pair_rows = 2 * levels
    row = lax.broadcasted_iota(jnp.int32, (pair_rows, lanes), 0)
    column = lax.broadcasted_iota(jnp.int32, (pair_rows, lanes), 1)
    level, level2 = row % levels, (column % lf) // fields
    depth = depth_ref[...]
    term = jnp.where(level2 > level, depth, jnp.where(level2 == level, 0.5 * depth, 0.0))
    fits = (row // levels == column // lf) & (column % fields == 0)
    term = jnp.where(fits, term, 0.0)
    high = term.astype(jnp.bfloat16)
    rest = (term - high.astype(jnp.float32)).astype(jnp.bfloat16)
    stacked = jnp.concatenate([high, rest], axis=0)

    for slot in range(slots):
        own_back(slot).wait()
        all_of(returned.at[pl.ds(0, n - 1)], recv_sem.at[1, slot]).wait()

    def gather_group(group, carry):
        start = pl.multiple_of(group * GROUP, GROUP)
        block = returned[:, pl.ds(start, GROUP), :].astype(jnp.float32)
        block = jnp.swapaxes(block, 0, 1)
        for pair in range(GROUP // 2):
            turn = group * GROUP + 2 * pair
            first, second = block[2 * pair], block[2 * pair + 1]
            real = jnp.where(low, first, pltpu.roll(second, lf, 1))
            imag = jnp.where(low, pltpu.roll(first, lf, 1), second)
            mixed = jnp.concatenate([real, imag], axis=0).astype(jnp.bfloat16)
            two = lax.dot_general(mixed, permute, TN, preferred_element_type=jnp.float32).astype(
                jnp.bfloat16
            )
            heights = jnp.dot(stacked, two, preferred_element_type=jnp.float32)
            heights = (heights[:pair_rows] + heights[pair_rows:]).astype(jnp.bfloat16)
            for h in range(2):
                lat = lat_of(turn + h)
                out_ref[lat] = two[h * lf : (h + 1) * lf]
                geo_ref[lat] = heights[h * levels : (h + 1) * levels]
        return carry

    lax.fori_loop(0, lats // GROUP, gather_group, 0)

    for slot in range(slots):
        all_of(outgoing.at[pl.ds(0, n - 1)], send_sem.at[0, slot]).wait()
        all_of(rows(results, slot * whole, many), send_sem.at[1, slot]).wait()


def geopotential_over(fields_out, layer_depth):
    contrib = layer_depth[None, :, None] * fields_out[:, :, 0, :].astype(jnp.float32)
    inside = jnp.cumsum(contrib[:, ::-1], axis=1)[:, ::-1]
    gathered = lax.all_gather(inside[:, 0], "lev")
    behind = jnp.arange(gathered.shape[0]) > lax.axis_index("lev")
    below = jnp.sum(jnp.where(behind[:, None, None], gathered, 0.0), axis=0)
    return (below[:, None, :] + inside - 0.5 * contrib).astype(jnp.bfloat16)


def on_device(fourier, owner, legendre, quad_weights, layer_depth):
    n = lax.axis_size("wave")
    lats, levels, fields, lanes = fourier.shape
    lf = levels * fields
    slots, _, half, north = legendre.shape
    waves = n * slots
    whole = n * lats
    assert lanes == 2 * waves and lanes == 2 * lf and whole == 2 * north
    own = jnp.concatenate([owner, owner + waves]).reshape(1, lanes)
    depth = jnp.tile(jnp.repeat(layer_depth, fields), 2).reshape(1, lanes)
    vmem = pl.BlockSpec(memory_space=pltpu.VMEM)
    fields_out, geopotential = pl.pallas_call(
        functools.partial(kernel, n, slots, 2 * half),
        out_shape=(
            jax.ShapeDtypeStruct((lats, lf, lanes), jnp.bfloat16),
            jax.ShapeDtypeStruct((lats, levels, lanes), jnp.bfloat16),
        ),
        in_specs=[vmem] * 4 + [pl.BlockSpec(memory_space=pl.ANY)],
        out_specs=(vmem, vmem),
        scratch_shapes=[
            pltpu.VMEM(legendre.shape, jnp.bfloat16),
            pltpu.VMEM((waves, lats, lanes), jnp.bfloat16),
            pltpu.VMEM((slots * whole, lanes), jnp.bfloat16),
            pltpu.VMEM((north, lanes), jnp.float32),
            pltpu.VMEM((2, north, lanes), jnp.bfloat16),
            pltpu.VMEM((2, half, lanes), jnp.bfloat16),
            pltpu.VMEM((slots * whole, lanes), jnp.bfloat16),
            pltpu.VMEM((waves, lats, lanes), jnp.bfloat16),
            pltpu.SemaphoreType.DMA((slots,)),
            pltpu.SemaphoreType.DMA((2, slots)),
            pltpu.SemaphoreType.DMA((2, slots)),
            pltpu.SemaphoreType.DMA((2, slots)),
        ],
        compiler_params=pltpu.CompilerParams(
            collective_id=0, has_side_effects=True, vmem_limit_bytes=48 * 2**20
        ),
        cost_estimate=pl.CostEstimate(
            flops=16 * slots * half * north * lanes,
            bytes_accessed=2 * legendre.size + 4 * fourier.size,
            transcendentals=0,
        ),
    )(
        fourier.reshape(lats, lf, lanes),
        own,
        depth,
        quad_weights.reshape(north // lanes, lanes),
        legendre,
    )
    fields_out = fields_out.reshape(lats, levels, fields, lanes)
    if lax.axis_size("lev") > 1:
        geopotential = geopotential_over(fields_out, layer_depth)
    return (fields_out, geopotential)


def solution(mesh):
    return jax.shard_map(
        on_device,
        mesh=mesh,
        in_specs=(P("wave", "lev", None, None), P(), P("wave", None, None, None), P(), P("lev")),
        out_specs=(P("wave", "lev", None, None), P("wave", "lev", None)),
        check_vma=False,
    )
```

```python
import functools

import jax
import jax.numpy as jnp
from jax import lax
from jax.experimental import pallas as pl
from jax.experimental.pallas import tpu as pltpu
from jax.sharding import PartitionSpec as P

MESH = pl.DeviceIdType.MESH
GROUP = 16
NT = (((1,), (1,)), ((), ()))
TN = (((0,), (0,)), ((), ()))


def kernel(
    n,
    slots,
    degrees,
    x_hbm,
    own_ref,
    depth_ref,
    weight_ref,
    table_hbm,
    out_hbm,
    geo_hbm,
    x_ref,
    out_ref,
    geo_ref,
    own_row,
    tables,
    outgoing,
    arrived,
    weights,
    folded,
    spectra,
    results,
    returned,
    x_sem,
    out_sem,
    table_sem,
    send_sem,
    recv_sem,
    own_sem,
):
    me = lax.axis_index("wave")
    lats, lf, lanes = x_ref.shape
    waves = n * slots
    half = tables.shape[2]
    north = tables.shape[3]
    whole = n * lats
    levels = geo_ref.shape[1]
    fields = lf // levels

    barrier = pltpu.get_barrier_semaphore()

    def greet(step, carry):
        other = lax.rem(me + step, n)
        pl.semaphore_signal(barrier, inc=1, device_id={"wave": other}, device_id_type=MESH)
        return carry

    lax.fori_loop(1, n, greet, 0)

    south = me >= n // 2
    groups = lats // GROUP

    def lats_of(group):
        return pl.ds(jnp.where(south, lats - GROUP - group * GROUP, group * GROUP), GROUP)

    def out_copies(group):
        piece = lats_of(group)
        return (
            pltpu.make_async_copy(out_ref.at[piece], out_hbm.at[piece], out_sem.at[0, group]),
            pltpu.make_async_copy(geo_ref.at[piece], geo_hbm.at[piece], out_sem.at[1, group]),
        )

    def x_copy(group):
        piece = lats_of(group)
        return pltpu.make_async_copy(x_hbm.at[piece], x_ref.at[piece], x_sem.at[group])

    for group in range(groups):
        x_copy(group).start()

    def table_copy(slot):
        return pltpu.make_async_copy(table_hbm.at[slot], tables.at[slot], table_sem.at[slot])

    for slot in range(slots):
        table_copy(slot).start()

    place = jnp.where(south, n // 2 + (n - 1 - me), me)

    def lat_of(turn):
        return jnp.where(south, lats - 1 - turn, turn)

    rows_i = lax.broadcasted_iota(jnp.int32, (lanes, lanes), 0)
    lane = lax.broadcasted_iota(jnp.int32, (1, lanes), 1)
    owner = jnp.zeros((1, lanes), jnp.int32)
    for wave in range(waves):
        owner = jnp.where(lane % waves == wave, own_ref[wave], owner)
    own_row[...] = owner + waves * (lane // waves)
    permute = jnp.where(rows_i == own_row[...], 1.0, 0.0).astype(jnp.bfloat16)
    low = lax.broadcasted_iota(jnp.int32, (waves, lanes), 1) < lf

    def scatter_group(group, carry):
        x_copy(group).wait()
        parts = []
        for pair in range(GROUP // 2):
            turn = group * GROUP + 2 * pair
            two = jnp.concatenate([x_ref[lat_of(turn)], x_ref[lat_of(turn + 1)]], axis=0)
            mixed = lax.dot_general(permute, two, NT, preferred_element_type=jnp.float32)
            real, imag = mixed[:waves], mixed[waves:]
            parts.append(jnp.where(low, real, pltpu.roll(imag, lf, 1)))
            parts.append(jnp.where(low, pltpu.roll(real, lf, 1), imag))
        block = jnp.swapaxes(jnp.stack(parts, axis=0), 0, 1)
        start = pl.multiple_of(group * GROUP, GROUP)
        outgoing[:, pl.ds(start, GROUP), :] = block.astype(jnp.bfloat16)
        return carry

    first = (groups + 1) // 2
    lax.fori_loop(0, first, scatter_group, 0)
    pl.semaphore_wait(barrier, n - 1)

    def rows(ref, start, count):
        return ref.at[pl.ds(pl.multiple_of(start, GROUP), count), :]

    def partner(turn):
        return lax.rem(
            me + jnp.where(lax.rem(turn, 2) == 0, n // 2 + turn // 2, (turn + 1) // 2), n
        )

    def send_out(slot, begin, count):
        target = rows(arrived, slot * whole + place * lats + begin, count)

        def one(turn, carry):
            other = partner(turn)
            pltpu.make_async_remote_copy(
                src_ref=outgoing.at[other * slots + slot, pl.ds(begin, count)],
                dst_ref=target,
                send_sem=send_sem.at[0, slot],
                recv_sem=recv_sem.at[0, slot],
                device_id={"wave": other},
                device_id_type=MESH,
            ).start()
            return carry

        lax.fori_loop(0, n - 1, one, 0)

    def own_out(slot):
        return pltpu.make_async_copy(
            outgoing.at[me * slots + slot],
            rows(arrived, slot * whole + place * lats, lats),
            own_sem.at[0, slot],
        )

    def place_of(other):
        return jnp.where(other >= n // 2, n // 2 + (n - 1 - other), other)

    def send_back(slot, begin, count, sem):
        def one(turn, carry):
            other = partner(turn)
            pltpu.make_async_remote_copy(
                src_ref=rows(results, slot * whole + place_of(other) * lats + begin, count),
                dst_ref=returned.at[me * slots + slot, pl.ds(begin, count)],
                send_sem=send_sem.at[1, slot],
                recv_sem=recv_sem.at[1, sem],
                device_id={"wave": other},
                device_id_type=MESH,
            ).start()
            return carry

        lax.fori_loop(0, n - 1, one, 0)

    def own_back(slot):
        return pltpu.make_async_copy(
            rows(results, slot * whole + place * lats, lats),
            returned.at[me * slots + slot],
            own_sem.at[1, slot],
        )

    def all_of(ref, sem):
        return pltpu.make_async_copy(ref, ref, sem)

    many = (n - 1) * lats
    early = first * GROUP
    send_out(0, 0, early)
    lax.fori_loop(first, groups, scatter_group, 0)
    send_out(0, early, lats - early)
    for slot in range(1, slots):
        send_out(slot, 0, lats)
    for slot in range(slots):
        own_out(slot).start()

    for group in range(north // lanes):
        row = weight_ref[group : group + 1, :]
        weights[group * lanes : (group + 1) * lanes, :] = jnp.transpose(
            jnp.broadcast_to(row, (lanes, lanes))
        )

    lengths = degrees - (lane * degrees) // waves
    span = 2 * lanes
    part = lanes

    for slot in range(slots):
        table_copy(slot).wait()
        own_out(slot).wait()
        all_of(rows(arrived, slot * whole, many), recv_sem.at[0, slot]).wait()

        def fold(index, carry, slot=slot):
            start = pl.multiple_of(index * span, span)
            upper = arrived[pl.ds(slot * whole + start, span), :].astype(jnp.float32)
            lower = arrived[pl.ds(slot * whole + north + start, span), :].astype(jnp.float32)
            scale = weights[pl.ds(start, span), :]
            folded[0, pl.ds(start, span), :] = (scale * (upper + lower)).astype(jnp.bfloat16)
            folded[1, pl.ds(start, span), :] = (scale * (upper - lower)).astype(jnp.bfloat16)
            return carry

        lax.fori_loop(0, north // span, fold, 0)
        mine = (own_row[...] == me * slots + slot) & (lane < waves)
        length = jnp.sum(jnp.where(mine, lengths, 0), axis=1, keepdims=True)

        def direct(index, carry, slot=slot, length=length):
            start = pl.multiple_of(index * part, part)
            degree = 2 * (start + lax.broadcasted_iota(jnp.int32, (part, lanes), 0))
            for parity in range(2):
                value = jnp.dot(
                    tables[slot, parity, pl.ds(start, part), :],
                    folded[parity],
                    preferred_element_type=jnp.float32,
                )
                value = jnp.where(degree + parity < length, value, 0.0)
                spectra[parity, pl.ds(start, part), :] = value.astype(jnp.bfloat16)
            return carry

        lax.fori_loop(0, half // part, direct, 0)

        def inverse(index, carry, slot=slot):
            start = pl.multiple_of(index * span, span)
            even, odd = (
                lax.dot_general(
                    tables[slot, parity, :, pl.ds(start, span)],
                    spectra[parity],
                    TN,
                    preferred_element_type=jnp.float32,
                )
                for parity in range(2)
            )
            results[pl.ds(slot * whole + start, span), :] = (even + odd).astype(jnp.bfloat16)
            results[pl.ds(slot * whole + north + start, span), :] = (even - odd).astype(
                jnp.bfloat16
            )
            return carry

        lax.fori_loop(0, north // span, inverse, 0)
        if slot < slots - 1:
            send_back(slot, 0, lats, slot)
        else:
            send_back(slot, 0, early, slot)
            send_back(slot, early, lats - early, slots)
        own_back(slot).start()

    pair_rows = 2 * levels
    row = lax.broadcasted_iota(jnp.int32, (pair_rows, lanes), 0)
    column = lax.broadcasted_iota(jnp.int32, (pair_rows, lanes), 1)
    level, level2 = row % levels, (column % lf) // fields
    depth = jnp.zeros((pair_rows, lanes), jnp.float32)
    for index in range(levels):
        depth = jnp.where(level2 == index, depth_ref[index], depth)
    term = jnp.where(level2 > level, depth, jnp.where(level2 == level, 0.5 * depth, 0.0))
    fits = (row // levels == column // lf) & (column % fields == 0)
    term = jnp.where(fits, term, 0.0)
    high = term.astype(jnp.bfloat16)
    rest = (term - high.astype(jnp.float32)).astype(jnp.bfloat16)
    stacked = jnp.concatenate([high, rest], axis=0)

    for slot in range(slots):
        own_back(slot).wait()
        count = lats if slot < slots - 1 else early
        all_of(returned.at[pl.ds(0, n - 1), pl.ds(0, count)], recv_sem.at[1, slot]).wait()

    def gather_group(group, carry):
        start = pl.multiple_of(group * GROUP, GROUP)
        block = returned[:, pl.ds(start, GROUP), :].astype(jnp.float32)
        block = jnp.swapaxes(block, 0, 1)
        for pair in range(GROUP // 2):
            turn = group * GROUP + 2 * pair
            first, second = block[2 * pair], block[2 * pair + 1]
            real = jnp.where(low, first, pltpu.roll(second, lf, 1))
            imag = jnp.where(low, pltpu.roll(first, lf, 1), second)
            mixed = jnp.concatenate([real, imag], axis=0).astype(jnp.bfloat16)
            two = lax.dot_general(mixed, permute, TN, preferred_element_type=jnp.float32).astype(
                jnp.bfloat16
            )
            heights = jnp.dot(stacked, two, preferred_element_type=jnp.float32)
            heights = (heights[:pair_rows] + heights[pair_rows:]).astype(jnp.bfloat16)
            for h in range(2):
                lat = lat_of(turn + h)
                out_ref[lat] = two[h * lf : (h + 1) * lf]
                geo_ref[lat] = heights[h * levels : (h + 1) * levels]
        for copy in out_copies(group):
            copy.start()
        return carry

    lax.fori_loop(0, first, gather_group, 0)
    all_of(returned.at[pl.ds(0, n - 1), pl.ds(early, lats - early)], recv_sem.at[1, slots]).wait()
    lax.fori_loop(first, groups, gather_group, 0)
    for group in range(groups):
        for copy in out_copies(group):
            copy.wait()

    for slot in range(slots):
        all_of(outgoing.at[pl.ds(0, n - 1)], send_sem.at[0, slot]).wait()
        all_of(rows(results, slot * whole, many), send_sem.at[1, slot]).wait()


def geopotential_over(fields_out, layer_depth):
    contrib = layer_depth[None, :, None] * fields_out[:, :, 0, :].astype(jnp.float32)
    inside = jnp.cumsum(contrib[:, ::-1], axis=1)[:, ::-1]
    gathered = lax.all_gather(inside[:, 0], "lev")
    behind = jnp.arange(gathered.shape[0]) > lax.axis_index("lev")
    below = jnp.sum(jnp.where(behind[:, None, None], gathered, 0.0), axis=0)
    return (below[:, None, :] + inside - 0.5 * contrib).astype(jnp.bfloat16)


def on_device(fourier, owner, legendre, quad_weights, layer_depth):
    n = lax.axis_size("wave")
    lats, levels, fields, lanes = fourier.shape
    lf = levels * fields
    slots, _, half, north = legendre.shape
    waves = n * slots
    whole = n * lats
    assert lanes == 2 * waves and lanes == 2 * lf and whole == 2 * north
    far = pl.BlockSpec(memory_space=pltpu.HBM)
    smem = pl.BlockSpec(memory_space=pltpu.SMEM)
    vmem = pl.BlockSpec(memory_space=pltpu.VMEM)
    fields_out, geopotential = pl.pallas_call(
        functools.partial(kernel, n, slots, 2 * half),
        out_shape=(
            jax.ShapeDtypeStruct((lats, lf, lanes), jnp.bfloat16),
            jax.ShapeDtypeStruct((lats, levels, lanes), jnp.bfloat16),
        ),
        in_specs=[far, smem, smem, vmem, far],
        out_specs=(far, far),
        scratch_shapes=[
            pltpu.VMEM((lats, lf, lanes), jnp.bfloat16),
            pltpu.VMEM((lats, lf, lanes), jnp.bfloat16),
            pltpu.VMEM((lats, levels, lanes), jnp.bfloat16),
            pltpu.VMEM((1, lanes), jnp.int32),
            pltpu.VMEM(legendre.shape, jnp.bfloat16),
            pltpu.VMEM((waves, lats, lanes), jnp.bfloat16),
            pltpu.VMEM((slots * whole, lanes), jnp.bfloat16),
            pltpu.VMEM((north, lanes), jnp.float32),
            pltpu.VMEM((2, north, lanes), jnp.bfloat16),
            pltpu.VMEM((2, half, lanes), jnp.bfloat16),
            pltpu.VMEM((slots * whole, lanes), jnp.bfloat16),
            pltpu.VMEM((waves, lats, lanes), jnp.bfloat16),
            pltpu.SemaphoreType.DMA((lats // GROUP,)),
            pltpu.SemaphoreType.DMA((2, lats // GROUP)),
            pltpu.SemaphoreType.DMA((slots,)),
            pltpu.SemaphoreType.DMA((2, slots)),
            pltpu.SemaphoreType.DMA((2, slots + 1)),
            pltpu.SemaphoreType.DMA((2, slots)),
        ],
        compiler_params=pltpu.CompilerParams(
            collective_id=0, has_side_effects=True, vmem_limit_bytes=60 * 2**20
        ),
        cost_estimate=pl.CostEstimate(
            flops=16 * slots * half * north * lanes,
            bytes_accessed=2 * legendre.size + 4 * fourier.size,
            transcendentals=0,
        ),
    )(
        fourier.reshape(lats, lf, lanes),
        owner,
        layer_depth,
        quad_weights.reshape(north // lanes, lanes),
        legendre,
    )
    fields_out = fields_out.reshape(lats, levels, fields, lanes)
    if lax.axis_size("lev") > 1:
        geopotential = geopotential_over(fields_out, layer_depth)
    return (fields_out, geopotential)


def solution(mesh):
    return jax.shard_map(
        on_device,
        mesh=mesh,
        in_specs=(P("wave", "lev", None, None), P(), P("wave", None, None, None), P(), P("lev")),
        out_specs=(P("wave", "lev", None, None), P("wave", "lev", None)),
        check_vma=False,
    )
```

```python
import functools

import jax
import jax.numpy as jnp
from jax import lax
from jax.experimental import pallas as pl
from jax.experimental.pallas import tpu as pltpu
from jax.sharding import PartitionSpec as P

MESH = pl.DeviceIdType.MESH
GROUP = 16
NT = (((1,), (1,)), ((), ()))
TN = (((0,), (0,)), ((), ()))


def kernel(
    n,
    slots,
    degrees,
    x_hbm,
    own_ref,
    depth_ref,
    weight_ref,
    table_hbm,
    out_hbm,
    geo_hbm,
    x_ref,
    out_ref,
    geo_ref,
    own_row,
    tables,
    turned,
    outgoing,
    arrived,
    weights,
    folded,
    spectra,
    results,
    returned,
    x_sem,
    out_sem,
    table_sem,
    send_sem,
    recv_sem,
    own_sem,
):
    me = lax.axis_index("wave")
    lats, lf, lanes = x_ref.shape
    waves = n * slots
    half = tables.shape[2]
    north = tables.shape[3]
    whole = n * lats
    levels = geo_ref.shape[1]
    fields = lf // levels

    barrier = pltpu.get_barrier_semaphore()

    def greet(step, carry):
        other = lax.rem(me + step, n)
        pl.semaphore_signal(barrier, inc=1, device_id={"wave": other}, device_id_type=MESH)
        return carry

    lax.fori_loop(1, n, greet, 0)

    south = me >= n // 2
    groups = lats // GROUP

    def lats_of(group):
        return pl.ds(jnp.where(south, lats - GROUP - group * GROUP, group * GROUP), GROUP)

    def out_copies(group):
        piece = lats_of(group)
        return (
            pltpu.make_async_copy(out_ref.at[piece], out_hbm.at[piece], out_sem.at[0, group]),
            pltpu.make_async_copy(geo_ref.at[piece], geo_hbm.at[piece], out_sem.at[1, group]),
        )

    def x_copy(group):
        piece = lats_of(group)
        return pltpu.make_async_copy(x_hbm.at[piece], x_ref.at[piece], x_sem.at[group])

    for group in range(groups):
        x_copy(group).start()

    def table_copy(slot):
        return pltpu.make_async_copy(table_hbm.at[slot], tables.at[slot], table_sem.at[slot])

    for slot in range(slots):
        table_copy(slot).start()

    place = jnp.where(south, n // 2 + (n - 1 - me), me)

    def lat_of(turn):
        return jnp.where(south, lats - 1 - turn, turn)

    rows_i = lax.broadcasted_iota(jnp.int32, (lanes, lanes), 0)
    lane = lax.broadcasted_iota(jnp.int32, (1, lanes), 1)
    owner = jnp.zeros((1, lanes), jnp.int32)
    for wave in range(waves):
        owner = jnp.where(lane % waves == wave, own_ref[wave], owner)
    own_row[...] = owner + waves * (lane // waves)
    permute = jnp.where(rows_i == own_row[...], 1.0, 0.0).astype(jnp.bfloat16)
    low = lax.broadcasted_iota(jnp.int32, (waves, lanes), 1) < lf

    def scatter_group(group, carry):
        x_copy(group).wait()
        parts = []
        for pair in range(GROUP // 2):
            turn = group * GROUP + 2 * pair
            two = jnp.concatenate([x_ref[lat_of(turn)], x_ref[lat_of(turn + 1)]], axis=0)
            mixed = lax.dot_general(permute, two, NT, preferred_element_type=jnp.float32)
            real, imag = mixed[:waves], mixed[waves:]
            parts.append(jnp.where(low, real, pltpu.roll(imag, lf, 1)))
            parts.append(jnp.where(low, pltpu.roll(real, lf, 1), imag))
        block = jnp.swapaxes(jnp.stack(parts, axis=0), 0, 1)
        start = pl.multiple_of(group * GROUP, GROUP)
        outgoing[:, pl.ds(start, GROUP), :] = block.astype(jnp.bfloat16)
        return carry

    first = (groups + 1) // 2
    lax.fori_loop(0, first, scatter_group, 0)
    pl.semaphore_wait(barrier, n - 1)

    def rows(ref, start, count):
        return ref.at[pl.ds(pl.multiple_of(start, GROUP), count), :]

    def partner(turn):
        return lax.rem(
            me + jnp.where(lax.rem(turn, 2) == 0, n // 2 + turn // 2, (turn + 1) // 2), n
        )

    def send_out(slot, begin, count):
        target = rows(arrived, slot * whole + place * lats + begin, count)

        def one(turn, carry):
            other = partner(turn)
            pltpu.make_async_remote_copy(
                src_ref=outgoing.at[other * slots + slot, pl.ds(begin, count)],
                dst_ref=target,
                send_sem=send_sem.at[0, slot],
                recv_sem=recv_sem.at[0, slot],
                device_id={"wave": other},
                device_id_type=MESH,
            ).start()
            return carry

        lax.fori_loop(0, n - 1, one, 0)

    def own_out(slot):
        return pltpu.make_async_copy(
            outgoing.at[me * slots + slot],
            rows(arrived, slot * whole + place * lats, lats),
            own_sem.at[0, slot],
        )

    def place_of(other):
        return jnp.where(other >= n // 2, n // 2 + (n - 1 - other), other)

    def send_back(slot, begin, count, sem):
        def one(turn, carry):
            other = partner(turn)
            pltpu.make_async_remote_copy(
                src_ref=rows(results, slot * whole + place_of(other) * lats + begin, count),
                dst_ref=returned.at[me * slots + slot, pl.ds(begin, count)],
                send_sem=send_sem.at[1, slot],
                recv_sem=recv_sem.at[1, sem],
                device_id={"wave": other},
                device_id_type=MESH,
            ).start()
            return carry

        lax.fori_loop(0, n - 1, one, 0)

    def own_back(slot):
        return pltpu.make_async_copy(
            rows(results, slot * whole + place * lats, lats),
            returned.at[me * slots + slot],
            own_sem.at[1, slot],
        )

    def all_of(ref, sem):
        return pltpu.make_async_copy(ref, ref, sem)

    many = (n - 1) * lats
    early = first * GROUP
    send_out(0, 0, early)
    lax.fori_loop(first, groups, scatter_group, 0)
    send_out(0, early, lats - early)
    for slot in range(1, slots):
        send_out(slot, 0, lats)
    for slot in range(slots):
        own_out(slot).start()

    for group in range(north // lanes):
        row = weight_ref[group : group + 1, :]
        weights[group * lanes : (group + 1) * lanes, :] = jnp.transpose(
            jnp.broadcast_to(row, (lanes, lanes))
        )

    lengths = degrees - (lane * degrees) // waves
    span = 2 * lanes
    part = lanes

    for slot in range(slots):
        table_copy(slot).wait()

        def turn_over(index, carry, slot=slot):
            start = pl.multiple_of(index * part, part)
            for parity in range(2):
                turned[slot, parity, pl.ds(start, part), :] = jnp.transpose(
                    tables[slot, parity, :, pl.ds(start, part)]
                )
            return carry

        lax.fori_loop(0, north // part, turn_over, 0)

    for slot in range(slots):
        own_out(slot).wait()
        all_of(rows(arrived, slot * whole, many), recv_sem.at[0, slot]).wait()

        def fold(index, carry, slot=slot):
            start = pl.multiple_of(index * span, span)
            upper = arrived[pl.ds(slot * whole + start, span), :].astype(jnp.float32)
            lower = arrived[pl.ds(slot * whole + north + start, span), :].astype(jnp.float32)
            scale = weights[pl.ds(start, span), :]
            folded[0, pl.ds(start, span), :] = (scale * (upper + lower)).astype(jnp.bfloat16)
            folded[1, pl.ds(start, span), :] = (scale * (upper - lower)).astype(jnp.bfloat16)
            return carry

        lax.fori_loop(0, north // span, fold, 0)
        mine = (own_row[...] == me * slots + slot) & (lane < waves)
        length = jnp.sum(jnp.where(mine, lengths, 0), axis=1, keepdims=True)

        def direct(index, carry, slot=slot, length=length):
            start = pl.multiple_of(index * part, part)
            degree = 2 * (start + lax.broadcasted_iota(jnp.int32, (part, lanes), 0))
            for parity in range(2):
                value = jnp.dot(
                    tables[slot, parity, pl.ds(start, part), :],
                    folded[parity],
                    preferred_element_type=jnp.float32,
                )
                value = jnp.where(degree + parity < length, value, 0.0)
                spectra[parity, pl.ds(start, part), :] = value.astype(jnp.bfloat16)
            return carry

        lax.fori_loop(0, half // part, direct, 0)

        def inverse(index, carry, slot=slot):
            start = pl.multiple_of(index * span, span)
            even, odd = (
                jnp.dot(
                    turned[slot, parity, pl.ds(start, span), :],
                    spectra[parity],
                    preferred_element_type=jnp.float32,
                )
                for parity in range(2)
            )
            results[pl.ds(slot * whole + start, span), :] = (even + odd).astype(jnp.bfloat16)
            results[pl.ds(slot * whole + north + start, span), :] = (even - odd).astype(
                jnp.bfloat16
            )
            return carry

        lax.fori_loop(0, north // span, inverse, 0)
        if slot < slots - 1:
            send_back(slot, 0, lats, slot)
        else:
            send_back(slot, 0, early, slot)
            send_back(slot, early, lats - early, slots)
        own_back(slot).start()

    pair_rows = 2 * levels
    row = lax.broadcasted_iota(jnp.int32, (pair_rows, lanes), 0)
    column = lax.broadcasted_iota(jnp.int32, (pair_rows, lanes), 1)
    level, level2 = row % levels, (column % lf) // fields
    depth = jnp.zeros((pair_rows, lanes), jnp.float32)
    for index in range(levels):
        depth = jnp.where(level2 == index, depth_ref[index], depth)
    term = jnp.where(level2 > level, depth, jnp.where(level2 == level, 0.5 * depth, 0.0))
    fits = (row // levels == column // lf) & (column % fields == 0)
    term = jnp.where(fits, term, 0.0)
    high = term.astype(jnp.bfloat16)
    rest = (term - high.astype(jnp.float32)).astype(jnp.bfloat16)
    stacked = jnp.concatenate([high, rest], axis=0)

    for slot in range(slots):
        own_back(slot).wait()
        count = lats if slot < slots - 1 else early
        all_of(returned.at[pl.ds(0, n - 1), pl.ds(0, count)], recv_sem.at[1, slot]).wait()

    def gather_group(group, carry):
        start = pl.multiple_of(group * GROUP, GROUP)
        block = returned[:, pl.ds(start, GROUP), :].astype(jnp.float32)
        block = jnp.swapaxes(block, 0, 1)
        for pair in range(GROUP // 2):
            turn = group * GROUP + 2 * pair
            first, second = block[2 * pair], block[2 * pair + 1]
            real = jnp.where(low, first, pltpu.roll(second, lf, 1))
            imag = jnp.where(low, pltpu.roll(first, lf, 1), second)
            mixed = jnp.concatenate([real, imag], axis=0).astype(jnp.bfloat16)
            two = lax.dot_general(mixed, permute, TN, preferred_element_type=jnp.float32).astype(
                jnp.bfloat16
            )
            heights = jnp.dot(stacked, two, preferred_element_type=jnp.float32)
            heights = (heights[:pair_rows] + heights[pair_rows:]).astype(jnp.bfloat16)
            for h in range(2):
                lat = lat_of(turn + h)
                out_ref[lat] = two[h * lf : (h + 1) * lf]
                geo_ref[lat] = heights[h * levels : (h + 1) * levels]
        for copy in out_copies(group):
            copy.start()
        return carry

    lax.fori_loop(0, first, gather_group, 0)
    all_of(returned.at[pl.ds(0, n - 1), pl.ds(early, lats - early)], recv_sem.at[1, slots]).wait()
    lax.fori_loop(first, groups, gather_group, 0)
    for group in range(groups):
        for copy in out_copies(group):
            copy.wait()

    for slot in range(slots):
        all_of(outgoing.at[pl.ds(0, n - 1)], send_sem.at[0, slot]).wait()
        all_of(rows(results, slot * whole, many), send_sem.at[1, slot]).wait()


def geopotential_over(fields_out, layer_depth):
    contrib = layer_depth[None, :, None] * fields_out[:, :, 0, :].astype(jnp.float32)
    inside = jnp.cumsum(contrib[:, ::-1], axis=1)[:, ::-1]
    gathered = lax.all_gather(inside[:, 0], "lev")
    behind = jnp.arange(gathered.shape[0]) > lax.axis_index("lev")
    below = jnp.sum(jnp.where(behind[:, None, None], gathered, 0.0), axis=0)
    return (below[:, None, :] + inside - 0.5 * contrib).astype(jnp.bfloat16)


def on_device(fourier, owner, legendre, quad_weights, layer_depth):
    n = lax.axis_size("wave")
    lats, levels, fields, lanes = fourier.shape
    lf = levels * fields
    slots, _, half, north = legendre.shape
    waves = n * slots
    whole = n * lats
    assert lanes == 2 * waves and lanes == 2 * lf and whole == 2 * north
    far = pl.BlockSpec(memory_space=pltpu.HBM)
    smem = pl.BlockSpec(memory_space=pltpu.SMEM)
    vmem = pl.BlockSpec(memory_space=pltpu.VMEM)
    fields_out, geopotential = pl.pallas_call(
        functools.partial(kernel, n, slots, 2 * half),
        out_shape=(
            jax.ShapeDtypeStruct((lats, lf, lanes), jnp.bfloat16),
            jax.ShapeDtypeStruct((lats, levels, lanes), jnp.bfloat16),
        ),
        in_specs=[far, smem, smem, vmem, far],
        out_specs=(far, far),
        scratch_shapes=[
            pltpu.VMEM((lats, lf, lanes), jnp.bfloat16),
            pltpu.VMEM((lats, lf, lanes), jnp.bfloat16),
            pltpu.VMEM((lats, levels, lanes), jnp.bfloat16),
            pltpu.VMEM((1, lanes), jnp.int32),
            pltpu.VMEM(legendre.shape, jnp.bfloat16),
            pltpu.VMEM((slots, 2, north, half), jnp.bfloat16),
            pltpu.VMEM((waves, lats, lanes), jnp.bfloat16),
            pltpu.VMEM((slots * whole, lanes), jnp.bfloat16),
            pltpu.VMEM((north, lanes), jnp.float32),
            pltpu.VMEM((2, north, lanes), jnp.bfloat16),
            pltpu.VMEM((2, half, lanes), jnp.bfloat16),
            pltpu.VMEM((slots * whole, lanes), jnp.bfloat16),
            pltpu.VMEM((waves, lats, lanes), jnp.bfloat16),
            pltpu.SemaphoreType.DMA((lats // GROUP,)),
            pltpu.SemaphoreType.DMA((2, lats // GROUP)),
            pltpu.SemaphoreType.DMA((slots,)),
            pltpu.SemaphoreType.DMA((2, slots)),
            pltpu.SemaphoreType.DMA((2, slots + 1)),
            pltpu.SemaphoreType.DMA((2, slots)),
        ],
        compiler_params=pltpu.CompilerParams(
            collective_id=0, has_side_effects=True, vmem_limit_bytes=52 * 2**20
        ),
        cost_estimate=pl.CostEstimate(
            flops=16 * slots * half * north * lanes,
            bytes_accessed=2 * legendre.size + 4 * fourier.size,
            transcendentals=0,
        ),
    )(
        fourier.reshape(lats, lf, lanes),
        owner,
        layer_depth,
        quad_weights.reshape(north // lanes, lanes),
        legendre,
    )
    fields_out = fields_out.reshape(lats, levels, fields, lanes)
    if lax.axis_size("lev") > 1:
        geopotential = geopotential_over(fields_out, layer_depth)
    return (fields_out, geopotential)


def solution(mesh):
    return jax.shard_map(
        on_device,
        mesh=mesh,
        in_specs=(P("wave", "lev", None, None), P(), P("wave", None, None, None), P(), P("lev")),
        out_specs=(P("wave", "lev", None, None), P("wave", "lev", None)),
        check_vma=False,
    )
```

```python
import functools

import jax
import jax.numpy as jnp
from jax import lax
from jax.experimental import pallas as pl
from jax.experimental.pallas import tpu as pltpu
from jax.sharding import PartitionSpec as P

MESH = pl.DeviceIdType.MESH
GROUP = 16
NT = (((1,), (1,)), ((), ()))
TN = (((0,), (0,)), ((), ()))


def kernel(
    n,
    slots,
    degrees,
    x_hbm,
    weight_ref,
    table_hbm,
    out_hbm,
    geo_hbm,
    x_ref,
    out_ref,
    geo_ref,
    own_row,
    tables,
    turned,
    outgoing,
    arrived,
    weights,
    folded,
    spectra,
    results,
    returned,
    x_sem,
    out_sem,
    table_sem,
    send_sem,
    recv_sem,
    own_sem,
):
    me = lax.axis_index("wave")
    lats, lf, lanes = x_ref.shape
    waves = n * slots
    half = tables.shape[2]
    north = tables.shape[3]
    whole = n * lats
    levels = geo_ref.shape[1]
    fields = lf // levels

    barrier = pltpu.get_barrier_semaphore()

    def greet(step, carry):
        other = lax.rem(me + step, n)
        pl.semaphore_signal(barrier, inc=1, device_id={"wave": other}, device_id_type=MESH)
        return carry

    lax.fori_loop(1, n, greet, 0)

    south = me >= n // 2
    groups = lats // GROUP

    def lats_of(group):
        return pl.ds(jnp.where(south, lats - GROUP - group * GROUP, group * GROUP), GROUP)

    def out_copies(group):
        piece = lats_of(group)
        return (
            pltpu.make_async_copy(out_ref.at[piece], out_hbm.at[piece], out_sem.at[0, group]),
            pltpu.make_async_copy(geo_ref.at[piece], geo_hbm.at[piece], out_sem.at[1, group]),
        )

    def x_copy(group):
        piece = lats_of(group)
        return pltpu.make_async_copy(x_hbm.at[piece], x_ref.at[piece], x_sem.at[group])

    for group in range(groups):
        x_copy(group).start()

    def table_copy(slot):
        return pltpu.make_async_copy(table_hbm.at[slot], tables.at[slot], table_sem.at[slot])

    for slot in range(slots):
        table_copy(slot).start()

    place = jnp.where(south, n // 2 + (n - 1 - me), me)

    def lat_of(turn):
        return jnp.where(south, lats - 1 - turn, turn)

    rows_i = lax.broadcasted_iota(jnp.int32, (lanes, lanes), 0)
    lane = lax.broadcasted_iota(jnp.int32, (1, lanes), 1)
    last_row = tables.shape[3] // lanes
    small = weight_ref[last_row : last_row + 1, :]
    owner = jnp.where(lane < waves, small, pltpu.roll(small, waves, 1)).astype(jnp.int32)
    own_row[...] = owner + waves * (lane // waves)
    permute = jnp.where(rows_i == own_row[...], 1.0, 0.0).astype(jnp.bfloat16)
    low = lax.broadcasted_iota(jnp.int32, (waves, lanes), 1) < lf

    def scatter_group(group, carry):
        x_copy(group).wait()
        parts = []
        for pair in range(GROUP // 2):
            turn = group * GROUP + 2 * pair
            two = jnp.concatenate([x_ref[lat_of(turn)], x_ref[lat_of(turn + 1)]], axis=0)
            mixed = lax.dot_general(permute, two, NT, preferred_element_type=jnp.float32)
            real, imag = mixed[:waves], mixed[waves:]
            parts.append(jnp.where(low, real, pltpu.roll(imag, lf, 1)))
            parts.append(jnp.where(low, pltpu.roll(real, lf, 1), imag))
        block = jnp.swapaxes(jnp.stack(parts, axis=0), 0, 1)
        start = pl.multiple_of(group * GROUP, GROUP)
        outgoing[:, pl.ds(start, GROUP), :] = block.astype(jnp.bfloat16)
        return carry

    first = (groups + 1) // 2
    lax.fori_loop(0, first, scatter_group, 0)
    pl.semaphore_wait(barrier, n - 1)

    def rows(ref, start, count):
        return ref.at[pl.ds(pl.multiple_of(start, GROUP), count), :]

    def partner(turn):
        return lax.rem(
            me + jnp.where(lax.rem(turn, 2) == 0, n // 2 + turn // 2, (turn + 1) // 2), n
        )

    def send_out(slot, begin, count):
        target = rows(arrived, slot * whole + place * lats + begin, count)

        def one(turn, carry):
            other = partner(turn)
            pltpu.make_async_remote_copy(
                src_ref=outgoing.at[other * slots + slot, pl.ds(begin, count)],
                dst_ref=target,
                send_sem=send_sem.at[0, slot],
                recv_sem=recv_sem.at[0, slot],
                device_id={"wave": other},
                device_id_type=MESH,
            ).start()
            return carry

        lax.fori_loop(0, n - 1, one, 0)

    def own_out(slot):
        return pltpu.make_async_copy(
            outgoing.at[me * slots + slot],
            rows(arrived, slot * whole + place * lats, lats),
            own_sem.at[0, slot],
        )

    def place_of(other):
        return jnp.where(other >= n // 2, n // 2 + (n - 1 - other), other)

    def send_back(slot, begin, count, sem):
        def one(turn, carry):
            other = partner(turn)
            pltpu.make_async_remote_copy(
                src_ref=rows(results, slot * whole + place_of(other) * lats + begin, count),
                dst_ref=returned.at[me * slots + slot, pl.ds(begin, count)],
                send_sem=send_sem.at[1, slot],
                recv_sem=recv_sem.at[1, sem],
                device_id={"wave": other},
                device_id_type=MESH,
            ).start()
            return carry

        lax.fori_loop(0, n - 1, one, 0)

    def own_back(slot):
        return pltpu.make_async_copy(
            rows(results, slot * whole + place * lats, lats),
            returned.at[me * slots + slot],
            own_sem.at[1, slot],
        )

    def all_of(ref, sem):
        return pltpu.make_async_copy(ref, ref, sem)

    many = (n - 1) * lats
    early = first * GROUP
    send_out(0, 0, early)
    lax.fori_loop(first, groups, scatter_group, 0)
    send_out(0, early, lats - early)
    for slot in range(1, slots):
        send_out(slot, 0, lats)
    for slot in range(slots):
        own_out(slot).start()

    for group in range(north // lanes):
        row = weight_ref[group : group + 1, :]
        weights[group * lanes : (group + 1) * lanes, :] = jnp.transpose(
            jnp.broadcast_to(row, (lanes, lanes))
        )

    lengths = degrees - (lane * degrees) // waves
    span = 2 * lanes
    part = lanes

    for slot in range(slots):
        table_copy(slot).wait()

        def turn_over(index, carry, slot=slot):
            start = pl.multiple_of(index * part, part)
            for parity in range(2):
                turned[slot, parity, pl.ds(start, part), :] = jnp.transpose(
                    tables[slot, parity, :, pl.ds(start, part)]
                )
            return carry

        lax.fori_loop(0, north // part, turn_over, 0)

    for slot in range(slots):
        own_out(slot).wait()
        all_of(rows(arrived, slot * whole, many), recv_sem.at[0, slot]).wait()

        def fold(index, carry, slot=slot):
            start = pl.multiple_of(index * span, span)
            upper = arrived[pl.ds(slot * whole + start, span), :].astype(jnp.float32)
            lower = arrived[pl.ds(slot * whole + north + start, span), :].astype(jnp.float32)
            scale = weights[pl.ds(start, span), :]
            folded[0, pl.ds(start, span), :] = (scale * (upper + lower)).astype(jnp.bfloat16)
            folded[1, pl.ds(start, span), :] = (scale * (upper - lower)).astype(jnp.bfloat16)
            return carry

        lax.fori_loop(0, north // span, fold, 0)
        mine = (own_row[...] == me * slots + slot) & (lane < waves)
        length = jnp.sum(jnp.where(mine, lengths, 0), axis=1, keepdims=True)

        def direct(index, carry, slot=slot, length=length):
            start = pl.multiple_of(index * part, part)
            degree = 2 * (start + lax.broadcasted_iota(jnp.int32, (part, lanes), 0))
            for parity in range(2):
                value = jnp.dot(
                    tables[slot, parity, pl.ds(start, part), :],
                    folded[parity],
                    preferred_element_type=jnp.float32,
                )
                value = jnp.where(degree + parity < length, value, 0.0)
                spectra[parity, pl.ds(start, part), :] = value.astype(jnp.bfloat16)
            return carry

        lax.fori_loop(0, half // part, direct, 0)

        def inverse(index, carry, slot=slot):
            start = pl.multiple_of(index * span, span)
            even, odd = (
                jnp.dot(
                    turned[slot, parity, pl.ds(start, span), :],
                    spectra[parity],
                    preferred_element_type=jnp.float32,
                )
                for parity in range(2)
            )
            results[pl.ds(slot * whole + start, span), :] = (even + odd).astype(jnp.bfloat16)
            results[pl.ds(slot * whole + north + start, span), :] = (even - odd).astype(
                jnp.bfloat16
            )
            return carry

        lax.fori_loop(0, north // span, inverse, 0)
        if slot < slots - 1:
            send_back(slot, 0, lats, slot)
        else:
            send_back(slot, 0, early, slot)
            send_back(slot, early, lats - early, slots)
        own_back(slot).start()

    pair_rows = 2 * levels
    row = lax.broadcasted_iota(jnp.int32, (pair_rows, lanes), 0)
    column = lax.broadcasted_iota(jnp.int32, (pair_rows, lanes), 1)
    level, level2 = row % levels, (column % lf) // fields
    depth = jnp.zeros((pair_rows, lanes), jnp.float32)
    for index in range(levels):
        value = jnp.sum(jnp.where(lane == waves + index, small, 0.0), axis=1, keepdims=True)
        depth = jnp.where(level2 == index, value, depth)
    term = jnp.where(level2 > level, depth, jnp.where(level2 == level, 0.5 * depth, 0.0))
    fits = (row // levels == column // lf) & (column % fields == 0)
    term = jnp.where(fits, term, 0.0)
    high = term.astype(jnp.bfloat16)
    rest = (term - high.astype(jnp.float32)).astype(jnp.bfloat16)
    stacked = jnp.concatenate([high, rest], axis=0)

    for slot in range(slots):
        own_back(slot).wait()
        count = lats if slot < slots - 1 else early
        all_of(returned.at[pl.ds(0, n - 1), pl.ds(0, count)], recv_sem.at[1, slot]).wait()

    def gather_group(group, carry):
        start = pl.multiple_of(group * GROUP, GROUP)
        block = returned[:, pl.ds(start, GROUP), :].astype(jnp.float32)
        block = jnp.swapaxes(block, 0, 1)
        for pair in range(GROUP // 2):
            turn = group * GROUP + 2 * pair
            first, second = block[2 * pair], block[2 * pair + 1]
            real = jnp.where(low, first, pltpu.roll(second, lf, 1))
            imag = jnp.where(low, pltpu.roll(first, lf, 1), second)
            mixed = jnp.concatenate([real, imag], axis=0).astype(jnp.bfloat16)
            two = lax.dot_general(mixed, permute, TN, preferred_element_type=jnp.float32).astype(
                jnp.bfloat16
            )
            heights = jnp.dot(stacked, two, preferred_element_type=jnp.float32)
            heights = (heights[:pair_rows] + heights[pair_rows:]).astype(jnp.bfloat16)
            for h in range(2):
                lat = lat_of(turn + h)
                out_ref[lat] = two[h * lf : (h + 1) * lf]
                geo_ref[lat] = heights[h * levels : (h + 1) * levels]
        for copy in out_copies(group):
            copy.start()
        return carry

    lax.fori_loop(0, first, gather_group, 0)
    all_of(returned.at[pl.ds(0, n - 1), pl.ds(early, lats - early)], recv_sem.at[1, slots]).wait()
    lax.fori_loop(first, groups, gather_group, 0)
    for group in range(groups):
        for copy in out_copies(group):
            copy.wait()

    for slot in range(slots):
        all_of(outgoing.at[pl.ds(0, n - 1)], send_sem.at[0, slot]).wait()
        all_of(rows(results, slot * whole, many), send_sem.at[1, slot]).wait()


def geopotential_over(fields_out, layer_depth):
    contrib = layer_depth[None, :, None] * fields_out[:, :, 0, :].astype(jnp.float32)
    inside = jnp.cumsum(contrib[:, ::-1], axis=1)[:, ::-1]
    gathered = lax.all_gather(inside[:, 0], "lev")
    behind = jnp.arange(gathered.shape[0]) > lax.axis_index("lev")
    below = jnp.sum(jnp.where(behind[:, None, None], gathered, 0.0), axis=0)
    return (below[:, None, :] + inside - 0.5 * contrib).astype(jnp.bfloat16)


def on_device(fourier, owner, legendre, quad_weights, layer_depth):
    n = lax.axis_size("wave")
    lats, levels, fields, lanes = fourier.shape
    lf = levels * fields
    slots, _, half, north = legendre.shape
    waves = n * slots
    whole = n * lats
    assert lanes == 2 * waves and lanes == 2 * lf and whole == 2 * north and levels <= waves
    far = pl.BlockSpec(memory_space=pltpu.HBM)
    packed_rows = north // lanes + 1
    packed_size = packed_rows * lanes

    def laid(values, start):
        after = packed_size - start - values.shape[0]
        zero = jnp.zeros((), values.dtype)
        return lax.pad(values, zero, [(start, after, 0)]).astype(jnp.float32)

    packed = laid(quad_weights, 0) + laid(owner, north) + laid(layer_depth, north + waves)
    vmem = pl.BlockSpec(memory_space=pltpu.VMEM)
    fields_out, geopotential = pl.pallas_call(
        functools.partial(kernel, n, slots, 2 * half),
        out_shape=(
            jax.ShapeDtypeStruct((lats, lf, lanes), jnp.bfloat16),
            jax.ShapeDtypeStruct((lats, levels, lanes), jnp.bfloat16),
        ),
        in_specs=[far, vmem, far],
        out_specs=(far, far),
        scratch_shapes=[
            pltpu.VMEM((lats, lf, lanes), jnp.bfloat16),
            pltpu.VMEM((lats, lf, lanes), jnp.bfloat16),
            pltpu.VMEM((lats, levels, lanes), jnp.bfloat16),
            pltpu.VMEM((1, lanes), jnp.int32),
            pltpu.VMEM(legendre.shape, jnp.bfloat16),
            pltpu.VMEM((slots, 2, north, half), jnp.bfloat16),
            pltpu.VMEM((waves, lats, lanes), jnp.bfloat16),
            pltpu.VMEM((slots * whole, lanes), jnp.bfloat16),
            pltpu.VMEM((north, lanes), jnp.float32),
            pltpu.VMEM((2, north, lanes), jnp.bfloat16),
            pltpu.VMEM((2, half, lanes), jnp.bfloat16),
            pltpu.VMEM((slots * whole, lanes), jnp.bfloat16),
            pltpu.VMEM((waves, lats, lanes), jnp.bfloat16),
            pltpu.SemaphoreType.DMA((lats // GROUP,)),
            pltpu.SemaphoreType.DMA((2, lats // GROUP)),
            pltpu.SemaphoreType.DMA((slots,)),
            pltpu.SemaphoreType.DMA((2, slots)),
            pltpu.SemaphoreType.DMA((2, slots + 1)),
            pltpu.SemaphoreType.DMA((2, slots)),
        ],
        compiler_params=pltpu.CompilerParams(
            collective_id=0, has_side_effects=True, vmem_limit_bytes=52 * 2**20
        ),
        cost_estimate=pl.CostEstimate(
            flops=16 * slots * half * north * lanes,
            bytes_accessed=2 * legendre.size + 4 * fourier.size,
            transcendentals=0,
        ),
    )(
        fourier.reshape(lats, lf, lanes),
        packed.reshape(packed_rows, lanes),
        legendre,
    )
    fields_out = fields_out.reshape(lats, levels, fields, lanes)
    if lax.axis_size("lev") > 1:
        geopotential = geopotential_over(fields_out, layer_depth)
    return (fields_out, geopotential)


def solution(mesh):
    return jax.shard_map(
        on_device,
        mesh=mesh,
        in_specs=(P("wave", "lev", None, None), P(), P("wave", None, None, None), P(), P("lev")),
        out_specs=(P("wave", "lev", None, None), P("wave", "lev", None)),
        check_vma=False,
    )
```
